1024 devices in a mesh: fsdp: 64 (over z, x), tp: 16 (over y, core).
Axes of the slice: x: 8, y: 8, z: 8, core: 2. Of those that a mesh axis runs over, the one named last changes fastest.
Arguments:
- momentum: float32 [7168, 18432], P('fsdp', 'tp'), may hold values from -6 to 6
- gradient: bfloat16 [7168, 18432], P('fsdp', 'tp'), may hold values from -6 to 6
- factor: float32 [18432, 448], P('tp'), may hold values from -0.046875 to 0.046875
Outputs:
- new_momentum: float32 [7168, 18432], P('fsdp', 'tp')
- update: float32 [7168, 18432], P('fsdp', 'tp')
- new_factor: float32 [18432, 448], P('tp')
The draws below stay inside these ranges and needn't reach their ends.
All inputs are finite; a program needn't handle non-finite values.
Results may differ from the reference program's by a relative error of at most 0.0003.
Values sent between devices are 32-bit elements; how exact they have to be, the bound alone decides.
A program may use at most 64 MiB of HBM per device.

```python
import math
import jax
import jax.numpy as jnp
from jax import lax

M_ROWS = 7168
N_COLS = 18432
RANK = 448


def levels(key, shape, cuts, low, largest):
    factor_of, own = 1.0, jax.random.fold_in(key, 6)
    for dim, blocks in cuts:
        heights = jnp.exp(jax.random.uniform(jax.random.fold_in(own, dim), (blocks,), jnp.float32, low / len(cuts), largest / len(cuts)))
        factor_of = factor_of * jnp.repeat(heights, shape[dim] // blocks).reshape([-1 if axis == dim else 1 for axis in range(len(shape))])
    return factor_of


def scatter_about(key, shape, width, most, shards=(), held_as=jnp.bfloat16):
    result = jax.random.normal(key, shape, jnp.float32) * width
    if len(shards) > 0:
        result = levels(key, shape, shards, -0.22, 0.18) * result
    return jnp.clip(result, min=-most, max=most).astype(held_as)


def setup_inputs(seed: int = 0) -> dict:
    seeds = jax.random.split(jax.random.key(seed), 4)
    momentum = scatter_about(seeds[0], (M_ROWS, N_COLS), 1.0, 6.0, ((0, 64), (1, 16)), jnp.float32)
    gradient = scatter_about(seeds[1], (M_ROWS, N_COLS), 1.0, 6.0, ((0, 64), (1, 16)))
    factor = scatter_about(seeds[2], (N_COLS, RANK), N_COLS ** -0.5, 0.046875, ((0, 16),), jnp.float32)
    return dict(momentum=momentum, gradient=gradient, factor=factor)


momentum_decay = 0.95
epsilon = 1e-08

def mult(left, right):
    return jnp.dot(left, right, precision=lax.Precision.HIGHEST)

def reference(momentum, gradient, factor):
    buffer = momentum + gradient.astype(jnp.float32)
    projected = mult(buffer, factor)
    inner = mult(projected.T, projected)
    triangle = jnp.linalg.cholesky(inner)
    orthonormal = jax.scipy.linalg.solve_triangular(triangle, projected.T, lower=True).T
    right = mult(buffer.T, orthonormal)
    column_norms = jnp.sqrt(lax.optimization_barrier(jnp.sum(right * right, axis=0)) + epsilon)
    new_factor = right / column_norms
    new_momentum = buffer - (1.0 - momentum_decay) * mult(orthonormal, (new_factor * column_norms).T)
    scale_factor = math.sqrt(M_ROWS * N_COLS / RANK)
    update = scale_factor * mult(orthonormal, new_factor.T)
    return (new_momentum, update, new_factor)
```

```python
import math

import jax
import jax.numpy as jnp
from jax import lax
from jax.experimental import pallas as pl
from jax.experimental.pallas import tpu as pltpu
from jax.sharding import PartitionSpec as P

MESH = pl.DeviceIdType.MESH
F32 = jnp.float32
BF16 = jnp.bfloat16
M_ROWS = 7168
N_COLS = 18432
RANK = 448
ROWS = 112
COLS = 1152
HALF = 56
PAD = 512
momentum_decay = 0.95
epsilon = 1e-08

STREAMS = (
    ("x", 0, 384, 4, 3),
    ("x", 384, 256, 3, 4),
    ("z", 640, 256, 4, 3),
    ("z", 896, 256, 3, 4),
)


def split(a):
    high = a.astype(BF16)
    return high, (a - high.astype(F32)).astype(BF16)


def dot3(a, b, dims):
    ah, al = split(a)
    bh, bl = split(b)

    def one(u, v):
        return lax.dot_general(u, v, (dims, ((), ())), preferred_element_type=F32)

    return one(ah, bh) + (one(ah, bl) + one(al, bh))


def dot_high(a, b, dims):
    return lax.dot_general(
        a, b, (dims, ((), ())), preferred_element_type=F32, precision=lax.Precision.HIGHEST
    )


class Place:
    def __init__(self):
        f, t = lax.axis_index("fsdp"), lax.axis_index("tp")
        self.at = dict(z=f // 8, x=f % 8, y=t // 2, core=t % 2)

    def device(self, **delta):
        at = {k: (v + delta.get(k, 0)) % (2 if k == "core" else 8) for k, v in self.at.items()}
        return (at["z"] * 8 + at["x"], at["y"] * 2 + at["core"])

    def step(self, axis, d):
        return (self.at[axis] + d) % 8


class Copies:
    def __init__(self, send_sem, recv_sem):
        self.send_sem, self.recv_sem, self.used, self.all = send_sem, recv_sem, 0, []

    def start(self, src, dst, device):
        n = self.used
        self.used += 1
        copy = pltpu.make_async_remote_copy(
            src_ref=src,
            dst_ref=dst,
            send_sem=self.send_sem.at[n],
            recv_sem=self.recv_sem.at[n],
            device_id=device,
            device_id_type=MESH,
        )
        copy.start()
        self.all.append(copy)
        return copy

    def finish(self):
        for copy in self.all:
            copy.wait_send()


def rows_at(start, size):
    return pl.ds(pl.multiple_of(start, 8), size)


SEMS = 200


def sums_kernel(
    mom_ref, grad_ref, fac_ref, p_ref, inner_ref, gt_ref,
    pp, pcore, ph, py, pfull, ip, ix, irx, irz, ifull, gp, gright, gleft, gs, gd, ga,
    send_sem, recv_sem,
):
    here = Place()
    z, x, y, core = (here.at[k] for k in ("z", "x", "y", "core"))
    t = y * 2 + core
    copies = Copies(send_sem, recv_sem)
    barrier = pltpu.get_barrier_semaphore()
    peers = [here.device(core=1)]
    for axis in ("x", "z", "y"):
        peers += [here.device(**{axis: d}) for d in range(1, 8)]
    for peer in peers:
        pl.semaphore_signal(barrier, inc=1, device_id=peer, device_id_type=MESH)

    buffer = mom_ref[...] + grad_ref[...].astype(F32)
    partial = dot3(buffer, fac_ref[...], ((1,), (0,)))
    pp[0, :HALF] = partial[:HALF]
    pp[1, :HALF] = partial[HALF:]
    pp[:, HALF:] = jnp.zeros((2, 8, RANK), F32)
    pl.semaphore_wait(barrier, len(peers))

    sibling = here.device(core=1)
    c = copies.start(pp.at[1 - core], pcore, sibling)
    c.wait_recv()
    ph[...] = pp[core] + pcore[...]
    cs = []
    for d in range(1, 8):
        cs.append(copies.start(ph.at[rows_at(8 * here.step("y", d), 8)], py.at[d - 1], here.device(y=d)))
    for c in cs:
        c.wait_recv()
    total = ph[rows_at(8 * y, 8), :]
    for d in range(7):
        total = total + py[d]
    pfull[core, rows_at(8 * y, 8), :] = total
    cs = []
    tile = pfull.at[core, rows_at(8 * y, 8)]
    for d in range(1, 8):
        cs.append(copies.start(tile, tile, here.device(y=d)))
    for c in cs:
        c.wait_recv()
    copies.start(pfull.at[core], pfull.at[core], sibling).wait_recv()
    projected = jnp.concatenate([pfull[0, :HALF], pfull[1, :HALF]], axis=0)
    p_ref[...] = projected

    ip[...] = jnp.zeros((PAD, PAD), F32)
    ip[:RANK, :RANK] = dot_high(projected, projected, ((0,), (0,)))

    def chunk(k):
        return (
            rows_at(32 * t + 8 * (k // 2), 8),
            pl.ds(pl.multiple_of(256 * (k % 2), 256), 256),
        )

    inner_x = []
    for d in range(1, 8):
        r, l = chunk(here.step("x", d))
        inner_x.append(copies.start(ip.at[r, l], irx.at[d - 1], here.device(x=d)))

    gp[...] = dot3(projected, buffer, ((0,), (0,)))
    arrived = {}

    def ring_send(s):
        for n, (axis, lane, lanes, rights, lefts) in enumerate(STREAMS):
            ls = pl.ds(lane, lanes)
            for sign, count, store in ((1, rights, gright), (-1, lefts, gleft)):
                if s > count:
                    continue
                own = rows_at(HALF * here.step(axis, sign * (count + 1 - s)), HALF)
                if s == 1:
                    src = gp.at[own, ls]
                else:
                    arrived[n, sign].wait_recv()
                    store[s - 2, :, ls] += gp[own, ls]
                    src = store.at[s - 2, :, ls]
                arrived[n, sign] = copies.start(src, store.at[s - 1, :, ls], here.device(**{axis: sign}))

    ring_send(1)
    for c in inner_x:
        c.wait_recv()
    r, l = chunk(x)
    total = ip[r, l]
    for d in range(7):
        total = total + irx[d]
    ix[...] = total
    inner_z = []
    for d in range(1, 8):
        inner_z.append(copies.start(ix, irz.at[d - 1], here.device(z=d)))
    ring_send(2)
    for c in inner_z:
        c.wait_recv()
    total = jnp.zeros((8, 256), F32)
    irz[7] = ix[...]
    for k in range(8):
        total = total + irz[(z - k + 7) % 8]
    mine = (rows_at(8 * (x // 2), 8), pl.ds(pl.multiple_of(256 * (x % 2), 256), 256))
    ifull[y, core, mine[0], mine[1]] = total
    inner_y = []
    part = ifull.at[y, core, mine[0], mine[1]]
    for d in range(1, 8):
        inner_y.append(copies.start(part, part, here.device(y=d)))
    ring_send(3)
    for c in inner_y:
        c.wait_recv()
    inner_x = []
    part = ifull.at[:, core, mine[0], mine[1]]
    for d in range(1, 8):
        inner_x.append(copies.start(part, part, here.device(x=d)))
    ring_send(4)

    final = []
    for n, (axis, lane, lanes, rights, lefts) in enumerate(STREAMS):
        ls = pl.ds(lane, lanes)
        arrived[n, 1].wait_recv()
        arrived[n, -1].wait_recv()
        own = rows_at(HALF * here.at[axis], HALF)
        gs[:HALF, ls] = gp[own, ls] + gright[rights - 1, :, ls] + gleft[lefts - 1, :, ls]
    gs[HALF:] = jnp.zeros((8, COLS), F32)
    for axis, ls in (("z", pl.ds(0, 640)), ("x", pl.ds(640, 512))):
        for d in range(1, 8):
            src = gs.at[rows_at(8 * here.step(axis, d), 8), ls]
            final.append(copies.start(src, gd.at[d - 1, :, ls], here.device(**{axis: d})))
    for c in inner_x:
        c.wait_recv()
    inner_core = copies.start(ifull.at[:, core], ifull.at[:, core], sibling)
    for c in final:
        c.wait_recv()
    back = []
    for ring, axis, ls in (("x", "z", pl.ds(0, 640)), ("z", "x", pl.ds(640, 512))):
        r = rows_at(8 * here.at[axis], 8)
        total = gs[r, ls]
        for d in range(7):
            total = total + gd[d, :, ls]
        ga[here.at[ring], r, ls] = total
        part = ga.at[here.at[ring], r, ls]
        for d in range(1, 8):
            back.append(copies.start(part, part, here.device(**{axis: d})))
    for c in back:
        c.wait_recv()
    for s in range(1, 5):
        for n, (axis, lane, lanes, rights, lefts) in enumerate(STREAMS):
            for sign, count in ((1, rights), (-1, lefts)):
                if s > 1 and s - 1 <= count:
                    arrived[n, sign].wait_recv()
                if s > count:
                    continue
                part = ga.at[here.step(axis, -sign * (s - 1)), pl.ds(0, HALF), pl.ds(lane, lanes)]
                arrived[n, sign] = copies.start(part, part, here.device(**{axis: sign}))
    for n, (axis, lane, lanes, rights, lefts) in enumerate(STREAMS):
        for sign, count in ((1, rights), (-1, lefts)):
            if count == 4:
                arrived[n, sign].wait_recv()
    inner_core.wait_recv()
    inner_ref[...] = ifull[...].reshape(PAD, PAD)[:RANK]
    for k in range(8):
        gt_ref[HALF * k : HALF * (k + 1), :] = ga[k, :HALF]
    copies.finish()


def factor_block(block):
    row = lax.broadcasted_iota(jnp.int32, (64, 64), 0)
    col = lax.broadcasted_iota(jnp.int32, (64, 64), 1)
    eye = jnp.where(row == col, 1.0, 0.0).astype(F32)
    both = jnp.concatenate([block, eye], axis=1)
    tiles = [both[8 * q : 8 * q + 8] for q in range(8)]
    sub = lax.broadcasted_iota(jnp.int32, (8, 128), 0)

    def lane(v, k):
        return jnp.broadcast_to(v[:, k : k + 1], (8, 128))

    def sublane(v, k):
        return jnp.broadcast_to(v[k : k + 1, :], (8, 128))

    for p in range(8):
        cols = {(q, k): lane(tiles[q], 8 * p + k) for q in range(p, 8) for k in range(8)}
        for k in range(8):
            pivot = sublane(cols[p, k], k)
            scale = lax.rsqrt(pivot)
            inverse = scale * scale
            line = sublane(tiles[p], k)
            lead = [sublane(cols[p, j], k) for j in range(k + 1, 8)]
            for q in range(p, 8):
                m = cols[q, k] * inverse
                if q == p:
                    m = jnp.where(sub > k, m, 0.0)
                tiles[q] = tiles[q] - m * line
                for j in range(k + 1, 8):
                    cols[q, j] = cols[q, j] - m * lead[j - k - 1]
            tiles[p] = jnp.where(sub == k, tiles[p] * scale, tiles[p])
    return jnp.concatenate(tiles, axis=0)


def factor_kernel(inner_ref, gt_ref, p_ref, q_ref, right_ref, sq_ref, work, tri):
    work[...] = inner_ref[:, :RANK]
    lanes = lax.broadcasted_iota(jnp.int32, (64, RANK), 1)
    for j in range(7):
        lo, hi = 64 * j, 64 * (j + 1)
        both = factor_block(work[lo:hi, lo:hi])
        inverse = both[:, 64:]
        rows = dot_high(inverse, work[lo:hi, :], ((1,), (0,)))
        parts = [inverse]
        if j > 0:
            parts.insert(0, rows[:, :lo])
        if j < 6:
            parts.append(rows[:, hi:])
        rows = jnp.concatenate(parts, axis=1)
        tri[lo:hi, :] = jnp.where(lanes < hi, rows, 0.0)
        if j < 6:
            down = dot_high(rows[:, hi:], rows, ((0,), (0,)))
            below = work[hi:, :]
            keep = lax.broadcasted_iota(jnp.int32, below.shape, 1)
            below = jnp.where((keep >= lo) & (keep < hi), 0.0, below)
            work[hi:, :] = below - down
    inverse = tri[...]
    q_ref[...] = dot3(p_ref[...], inverse, ((1,), (1,)))
    right = dot3(gt_ref[...], inverse, ((0,), (1,)))
    right_ref[...] = right
    sq_ref[...] = jnp.broadcast_to(jnp.sum(right * right, axis=0, keepdims=True), (8, RANK))


def norms_kernel(sq_ref, out_ref, mine, pair, ys, send_sem, recv_sem):
    here = Place()
    copies = Copies(send_sem, recv_sem)
    barrier = pltpu.get_barrier_semaphore()
    peers = [here.device(core=1)] + [here.device(y=d) for d in range(1, 8)]
    for peer in peers:
        pl.semaphore_signal(barrier, inc=1, device_id=peer, device_id_type=MESH)
    mine[...] = sq_ref[...]
    pl.semaphore_wait(barrier, len(peers))
    copies.start(mine, pair, here.device(core=1)).wait_recv()
    ys[7] = mine[...] + pair[...]
    cs = [copies.start(ys.at[7], ys.at[d - 1], here.device(y=d)) for d in range(1, 8)]
    for c in cs:
        c.wait_recv()
    total = jnp.zeros((8, RANK), F32)
    for k in range(8):
        total = total + ys[(here.at["y"] - k + 7) % 8]
    out_ref[...] = total
    copies.finish()


def outputs_kernel(mom_ref, grad_ref, q_ref, right_ref, sq_ref, nm_ref, up_ref, nf_ref):
    inverse = lax.rsqrt(sq_ref[0:1, :] + epsilon)
    right = right_ref[...]
    nf_ref[...] = right * inverse
    rh, rl = split(right)
    q = q_ref[...]
    scale_factor = math.sqrt(M_ROWS * N_COLS / RANK)
    qh, ql = split(q * (scale_factor * inverse))

    def one(u, v):
        return lax.dot_general(u, v, (((1,), (1,)), ((), ())), preferred_element_type=F32)

    up_ref[...] = one(qh, rh) + (one(qh, rl) + one(ql, rh))
    buffer = mom_ref[...] + grad_ref[...].astype(F32)
    nm_ref[...] = buffer - one((q * (1.0 - momentum_decay)).astype(BF16), rh)


def shape(*dims):
    return jax.ShapeDtypeStruct(dims, F32)


VM = pl.BlockSpec(memory_space=pltpu.VMEM)
LIMIT = 48 * 1024 * 1024


def per_device(momentum, gradient, factor):
    scratch = [
        (2, 64, RANK), (64, RANK), (64, RANK), (7, 8, RANK), (2, 64, RANK),
        (PAD, PAD), (8, 256), (7, 8, 256), (8, 8, 256), (8, 2, 32, PAD),
        (RANK, COLS), (4, HALF, COLS), (4, HALF, COLS), (64, COLS), (7, 8, COLS), (8, 64, COLS),
    ]
    projected, inner, gt = pl.pallas_call(
        sums_kernel,
        out_shape=(shape(ROWS, RANK), shape(RANK, PAD), shape(RANK, COLS)),
        in_specs=[VM] * 3,
        out_specs=(VM,) * 3,
        scratch_shapes=[pltpu.VMEM(s, F32) for s in scratch]
        + [pltpu.SemaphoreType.DMA((SEMS,)), pltpu.SemaphoreType.DMA((SEMS,))],
        compiler_params=pltpu.CompilerParams(
            collective_id=0, has_side_effects=True, vmem_limit_bytes=LIMIT
        ),
        name="sums",
    )(momentum, gradient, factor)
    q, right, squares = pl.pallas_call(
        factor_kernel,
        out_shape=(shape(ROWS, RANK), shape(COLS, RANK), shape(8, RANK)),
        in_specs=[VM] * 3,
        out_specs=(VM,) * 3,
        scratch_shapes=[pltpu.VMEM((RANK, RANK), F32), pltpu.VMEM((RANK, RANK), F32)],
        compiler_params=pltpu.CompilerParams(vmem_limit_bytes=LIMIT),
        name="triangle",
    )(inner, gt, projected)
    squares = pl.pallas_call(
        norms_kernel,
        out_shape=shape(8, RANK),
        in_specs=[VM],
        out_specs=VM,
        scratch_shapes=[pltpu.VMEM((8, RANK), F32), pltpu.VMEM((8, RANK), F32), pltpu.VMEM((8, 8, RANK), F32)]
        + [pltpu.SemaphoreType.DMA((8,)), pltpu.SemaphoreType.DMA((8,))],
        compiler_params=pltpu.CompilerParams(
            collective_id=1, has_side_effects=True, vmem_limit_bytes=LIMIT
        ),
        name="norms",
    )(squares)
    return pl.pallas_call(
        outputs_kernel,
        out_shape=(shape(ROWS, COLS), shape(ROWS, COLS), shape(COLS, RANK)),
        in_specs=[VM] * 5,
        out_specs=(VM,) * 3,
        compiler_params=pltpu.CompilerParams(vmem_limit_bytes=LIMIT),
        name="outputs",
    )(momentum, gradient, q, right, squares)


def solution(mesh):
    in_specs = (P("fsdp", "tp"), P("fsdp", "tp"), P("tp", None))
    out_specs = (P("fsdp", "tp"), P("fsdp", "tp"), P("tp", None))
    return jax.shard_map(
        per_device, mesh=mesh, in_specs=in_specs, out_specs=out_specs, check_vma=False
    )
```

```python
import math

import jax
import jax.numpy as jnp
from jax import lax
from jax.experimental import pallas as pl
from jax.experimental.pallas import tpu as pltpu
from jax.sharding import PartitionSpec as P

MESH = pl.DeviceIdType.MESH
F32 = jnp.float32
BF16 = jnp.bfloat16
M_ROWS = 7168
N_COLS = 18432
RANK = 448
ROWS = 112
COLS = 1152
HALF = 56
PAD = 512
momentum_decay = 0.95
epsilon = 1e-08

GROUPS = (
    (("x", 0, 384, 1), ("z", 640, 256, 1)),
    (("x", 384, 256, -1), ("z", 896, 256, -1)),
)


def split(a):
    high = a.astype(BF16)
    return high, (a - high.astype(F32)).astype(BF16)


def dot3(a, b, dims):
    ah, al = split(a)
    bh, bl = split(b)

    def one(u, v):
        return lax.dot_general(u, v, (dims, ((), ())), preferred_element_type=F32)

    return one(ah, bh) + (one(ah, bl) + one(al, bh))


def dot_high(a, b, dims):
    return lax.dot_general(
        a, b, (dims, ((), ())), preferred_element_type=F32, precision=lax.Precision.HIGHEST
    )


class Place:
    def __init__(self):
        f, t = lax.axis_index("fsdp"), lax.axis_index("tp")
        eight, two = jnp.int32(8), jnp.int32(2)
        self.at = dict(z=lax.div(f, eight), x=lax.rem(f, eight), y=lax.div(t, two), core=lax.rem(t, two))
        self.steps = {(k, d): lax.rem(v + d, eight) for k, v in self.at.items() for d in range(8)}
        z, x, y, core = (self.at[k] for k in ("z", "x", "y", "core"))
        self.devices = {}
        for d in range(1, 8):
            self.devices["z", d] = (self.steps["z", d] * 8 + x, t)
            self.devices["x", d] = (z * 8 + self.steps["x", d], t)
            self.devices["y", d] = (f, self.steps["y", d] * 2 + core)
        self.devices["core", 1] = (f, y * 2 + 1 - core)

    def device(self, **delta):
        ((axis, d),) = delta.items()
        return self.devices[axis, d % 8]

    def shift(self, at, k):
        return lax.rem(at + (15 - k), jnp.int32(8))

    def step(self, axis, d):
        return self.steps[axis, d % 8]


class Copies:
    def __init__(self, send_sem, recv_sem):
        self.send_sem, self.recv_sem, self.used, self.all = send_sem, recv_sem, 0, []

    def start(self, src, dst, device):
        n = self.used
        self.used += 1
        copy = pltpu.make_async_remote_copy(
            src_ref=src,
            dst_ref=dst,
            send_sem=self.send_sem.at[n],
            recv_sem=self.recv_sem.at[n],
            device_id=device,
            device_id_type=MESH,
        )
        copy.start()
        self.all.append(copy)
        return copy

    def finish(self):
        for copy in self.all:
            copy.wait_send()
        self.all = []


def rows_at(start, size):
    return pl.ds(pl.multiple_of(start, 8), size)


SEMS = 200
STOP = 0
ORDER = "iabiabiabab"
TURNS = {14: "a", 22: "b", 36: "a", 44: "b"}


def sums_kernel(
    mom, grad, fac, q_ref, right_ref, sq_ref,
    pp, pcore, ph, py, pfull, ip, ix, irx, irz, ifull, gp, gr, gs, gd, ga,
    upper, tri, mine, pair, ys, slab_send, slab_recv, send_sem, recv_sem,
):
    here = Place()
    z, x, y, core = (here.at[k] for k in ("z", "x", "y", "core"))
    t = y * 2 + core
    copies = Copies(send_sem, recv_sem)
    barrier = pltpu.get_barrier_semaphore()
    sibling = here.device(core=1)
    peers = [sibling]
    for axis in ("y", "x", "z"):
        peers += [here.device(**{axis: d}) for d in range(1, 8)]
    for peer in peers:
        pl.semaphore_signal(barrier, inc=1, device_id=peer, device_id_type=MESH)
    ip[...] = jnp.zeros((PAD, PAD), F32)
    gs[...] = jnp.zeros((64, COLS), F32)
    pp[:, HALF:] = jnp.zeros((2, 8, RANK), F32)

    buffer = mom[...] + grad[...].astype(F32)
    partial = dot3(buffer, fac[...], ((1,), (1,)))
    pp[0, :HALF] = partial[:HALF]
    pp[1, :HALF] = partial[HALF:]
    pl.semaphore_wait(barrier, len(peers))
    if STOP == 1:
        return

    copies.start(pp.at[1 - core], pcore, sibling).wait_recv()
    ph[...] = pp[core] + pcore[...]
    cs = []
    for d in range(1, 8):
        cs.append(copies.start(ph.at[rows_at(8 * here.step("y", d), 8)], py.at[d - 1], here.device(y=d)))
    total = ph[rows_at(8 * y, 8), :]
    for d, c in enumerate(cs):
        c.wait_recv()
        total = total + py[d]
    pfull[core, rows_at(8 * y, 8), :] = total
    cs = []
    tile = pfull.at[core, rows_at(8 * y, 8)]
    for d in range(1, 8):
        cs.append(copies.start(tile, tile, here.device(y=d)))
    for c in cs:
        c.wait_recv()
    copies.start(pfull.at[core], pfull.at[core], sibling).wait_recv()
    if STOP == 2:
        copies.finish()
        return

    projected = jnp.concatenate([pfull[0, :HALF], pfull[1, :HALF], jnp.zeros((16, RANK), F32)], axis=0)
    across = jnp.transpose(projected)
    ip[:RANK, :RANK] = dot_high(across, projected, ((1,), (0,)))

    def chunk(k):
        return (
            rows_at(32 * t + 8 * lax.div(k, jnp.int32(2)), 8),
            pl.ds(pl.multiple_of(256 * lax.rem(k, jnp.int32(2)), 256), 256),
        )

    def inner_sum():
        cs = []
        for d in range(1, 8):
            r, l = chunk(here.step("x", d))
            cs.append(copies.start(ip.at[r, l], irx.at[d - 1], here.device(x=d)))
        yield
        r, l = chunk(x)
        total = ip[r, l]
        for d, c in enumerate(cs):
            c.wait_recv()
            total = total + irx[d]
        ix[...] = total
        cs = [copies.start(ix, irz.at[d - 1], here.device(z=d)) for d in range(1, 8)]
        yield
        for c in cs:
            c.wait_recv()
        total = jnp.zeros((8, 256), F32)
        irz[7] = ix[...]
        for k in range(8):
            total = total + irz[here.shift(z, k)]
        r, l = rows_at(8 * lax.div(x, jnp.int32(2)), 8), pl.ds(pl.multiple_of(256 * lax.rem(x, jnp.int32(2)), 256), 256)
        ifull[y, core, r, l] = total
        part = ifull.at[y, core, r, l]
        cs = [copies.start(part, part, here.device(x=d)) for d in range(1, 8)]
        yield
        for c in cs:
            c.wait_recv()
        @pl.when(y < 7)
        def _():
            for d in range(1, 8):
                slab(y, d).start()

        yield

    def slab(place, d=1):
        part = ifull.at[place, core]
        return pltpu.make_async_remote_copy(
            src_ref=part,
            dst_ref=part,
            send_sem=slab_send.at[d - 1],
            recv_sem=slab_recv.at[place],
            device_id=here.device(y=d),
            device_id_type=MESH,
        )

    swaps = {}

    def fetch(j):
        @pl.when(y != j)
        def _():
            slab(j).wait_recv()

        part = ifull.at[j, core]
        swaps[j] = copies.start(part, part, sibling)

    def block_rows(j):
        swaps[j].wait_recv()
        return ifull[j].reshape(64, PAD)[:, :RANK]

    def outer_sum(group):
        def own(axis, d, ls):
            return gp.at[rows_at(HALF * here.step(axis, d), HALF), ls]

        got = []
        for axis, lane, lanes, way in group:
            ls = pl.ds(lane, lanes)
            got.append({
                (slot, by): copies.start(own(axis, to, ls), gr.at[slot, :, ls], here.device(**{axis: by}))
                for slot, to, by in ((0, 3, 1), (1, -3, -1), (2, 4, 2 * way), (3, 1, 1), (4, -1, -1))
            })
        yield
        for (axis, lane, lanes, way), arrived in zip(group, got):
            ls = pl.ds(lane, lanes)
            for (slot, by), c in arrived.items():
                if slot < 3:
                    c.wait_recv()
            for slot, by in ((0, 2), (1, -2)):
                total = gr[slot, :, ls] + own(axis, by, ls)[...]
                if by == 2 * way:
                    total = total + gr[2, :, ls]
                gr[slot, :, ls] = total
                arrived[slot + 5, by] = copies.start(
                    gr.at[slot, :, ls], gr.at[slot + 5, :, ls], here.device(**{axis: by})
                )
        yield
        cs = {}
        for n, ((axis, lane, lanes, way), arrived) in enumerate(zip(group, got)):
            ls = pl.ds(lane, lanes)
            total = own(axis, 0, ls)[...]
            for (slot, by), c in arrived.items():
                if slot >= 3:
                    c.wait_recv()
                    total = total + gr[slot, :, ls]
            gs[:HALF, ls] = total
            other = "z" if axis == "x" else "x"
            for d in (4, 3, 5, 2, 6, 1, 7):
                src = gs.at[rows_at(8 * here.step(other, d), 8), ls]
                cs[n, d] = copies.start(src, gd.at[d - 1, :, ls], here.device(**{other: d}))
        yield
        back = []
        for n, (axis, lane, lanes, way) in enumerate(group):
            ls = pl.ds(lane, lanes)
            other = "z" if axis == "x" else "x"
            r = rows_at(8 * here.at[other], 8)
            total = gs[r, ls]
            for d in range(1, 8):
                cs[n, d].wait_recv()
                total = total + gd[d - 1, :, ls]
            ga[here.at[axis], r, ls] = total
            part = ga.at[here.at[axis], r, ls]
            back += [copies.start(part, part, here.device(**{other: d})) for d in (4, 3, 5, 2, 6, 1, 7)]
        yield

        def pass_on(axis, place, by, ls):
            part = ga.at[here.step(axis, place), pl.ds(0, HALF), ls]
            return copies.start(part, part, here.device(**{axis: by}))

        for c in back:
            c.wait_recv()
        got = []
        for axis, lane, lanes, way in group:
            got.append([pass_on(axis, 0, by, pl.ds(lane, lanes)) for by in (2, -2, 1, -1)])
        yield
        for (axis, lane, lanes, way), arrived in zip(group, got):
            arrived[0].wait_recv()
            arrived[1].wait_recv()
            for place, by in ((2, -1), (-2, 1), (-2 * way, 2 * way)):
                arrived.append(pass_on(axis, place, by, pl.ds(lane, lanes)))
        yield
        for arrived in got:
            for c in arrived[2:]:
                c.wait_recv()
        yield

    inner_steps, outer_steps = inner_sum(), [outer_sum(group) for group in GROUPS]
    todo = dict(i=inner_steps, a=outer_steps[0], b=outer_steps[1])
    pa, pb = split(across)
    padded = jnp.concatenate([buffer, jnp.zeros((16, COLS), F32)], axis=0)
    bh, bl = split(padded)

    def one(u, v):
        return jnp.dot(u, v, preferred_element_type=F32)

    next(inner_steps)
    for n, group in enumerate(GROUPS):
        for axis, lane, lanes, way in group:
            ls = slice(lane, lane + lanes)
            gp[:, ls] = one(pa, bh[:, ls]) + (one(pa, bl[:, ls]) + one(pb, bh[:, ls]))
        if STOP != 3:
            next(outer_steps[n])
    for name in ORDER:
        if STOP != 3 or name == "i":
            next(todo[name])
    fetch(0)
    for n, _ in enumerate(factor(block_rows, upper, tri) if STOP == 0 else range(56)):
        if n % 8 == 3 and n < 48:
            fetch(n // 8 + 1)
        if n in TURNS and STOP != 3:
            next(todo[TURNS[n]])
    if STOP > 0:
        for j in range(7):
            swaps[j].wait_recv()
        copies.finish()

        @pl.when(y < 7)
        def _():
            for d in range(1, 8):
                slab(y, d).wait_send()

        return
    inverse = tri[...]
    grown = jnp.concatenate([ga[k, :HALF] for k in range(8)], axis=0)
    right = dot3(inverse, grown, ((1,), (0,)))
    total = right[:, :128] * right[:, :128]
    for k in range(1, 9):
        total = total + right[:, 128 * k : 128 * (k + 1)] * right[:, 128 * k : 128 * (k + 1)]
    total = jnp.concatenate([total, jnp.zeros((PAD - RANK, 128), F32)], axis=0)
    total = jnp.sum(jnp.transpose(total), axis=0, keepdims=True)
    mine[...] = jnp.concatenate(
        [total[:, 128 * k : 128 * (k + 1)] for k in range(4)] + [jnp.zeros((4, 128), F32)], axis=0
    )
    c = copies.start(mine, pair, sibling)
    right_ref[...] = right
    c.wait_recv()
    ys[7] = mine[...] + pair[...]
    cs = [copies.start(ys.at[7], ys.at[d - 1], here.device(y=d)) for d in range(1, 8)]
    q_ref[...] = dot3(projected[:ROWS], inverse, ((1,), (1,)))
    copies.finish()

    @pl.when(y < 7)
    def _():
        for d in range(1, 8):
            slab(y, d).wait_send()

    for c in cs:
        c.wait_recv()
    total = jnp.zeros((8, 128), F32)
    for k in range(8):
        total = total + ys[here.shift(y, k)]
    sq_ref[...] = total
    copies.finish()


def factor_block(block):
    row = lax.broadcasted_iota(jnp.int32, (64, 64), 0)
    col = lax.broadcasted_iota(jnp.int32, (64, 64), 1)
    rest = jnp.concatenate([block, jnp.where(row == col, 1.0, 0.0).astype(F32)], axis=1)
    done = []
    for p in range(8):
        n = 64 - 8 * p
        below = lax.broadcasted_iota(jnp.int32, (n, 128), 0)
        cols = jnp.stack([jnp.broadcast_to(rest[:, 8 * p + k : 8 * p + k + 1], (n, 128)) for k in range(8)])
        for k in range(8):
            scale = lax.rsqrt(cols[0, k : k + 1])
            m = jnp.where(below > k, cols[0] * (scale * scale), 0.0)
            line = rest[k : k + 1]
            done.append(line * scale)
            rest = rest - m * line
            if k < 7:
                cols = cols[1:] - m[None] * cols[1:, k : k + 1]
        rest = rest[8:]
        yield None
    yield jnp.concatenate(done, axis=0)


def factor(block_rows, upper, tri):
    lanes = lax.broadcasted_iota(jnp.int32, (64, RANK), 1)
    for j in range(7):
        lo, hi = 64 * j, 64 * (j + 1)
        block = block_rows(j)
        if j > 0:
            before = lax.broadcasted_iota(jnp.int32, (lo, RANK), 1)
            down = jnp.where(before < lo, tri[:lo, :], upper[:lo, :])
            block = jnp.where(lanes < lo, 0.0, block) - dot_high(upper[:lo, lo:hi], down, ((0,), (0,)))
        for both in factor_block(block[:, lo:hi]):
            if both is None:
                yield None
        inverse = both[:, 64:]
        rows = dot_high(inverse, block, ((1,), (0,)))
        upper[lo:hi, :] = rows
        parts = [inverse]
        if j > 0:
            parts.insert(0, rows[:, :lo])
        if j < 6:
            parts.append(jnp.zeros((64, RANK - hi), F32))
        tri[lo:hi, :] = jnp.concatenate(parts, axis=1)


def outputs_kernel(mom_ref, grad_ref, q_ref, right_ref, sq_ref, nm_ref, up_ref, nf_ref):
    inverse = lax.rsqrt(sq_ref[...] + epsilon)
    inverse = jnp.concatenate([inverse[k : k + 1] for k in range(4)], axis=1)
    column = jnp.transpose(jnp.broadcast_to(inverse, (128, PAD)))[:RANK, 0:1]
    right = right_ref[...]
    nf_ref[...] = right * column
    rh, rl = split(right)
    q = q_ref[...]
    scale_factor = math.sqrt(M_ROWS * N_COLS / RANK)
    qh, ql = split(q * (scale_factor * inverse[:, :RANK]))

    def one(u, v):
        return jnp.dot(u, v, preferred_element_type=F32)

    up_ref[...] = one(qh, rh) + (one(qh, rl) + one(ql, rh))
    buffer = mom_ref[...] + grad_ref[...].astype(F32)
    nm_ref[...] = buffer - one((q * (1.0 - momentum_decay)).astype(BF16), rh)


def shape(*dims):
    return jax.ShapeDtypeStruct(dims, F32)


VM = pl.BlockSpec(memory_space=pltpu.VMEM)
LIMIT = 48 * 1024 * 1024


def per_device(momentum, gradient, factor_rows):
    scratch = [
        (2, 64, RANK), (64, RANK), (64, RANK), (7, 8, RANK), (2, 64, RANK),
        (PAD, PAD), (8, 256), (7, 8, 256), (8, 8, 256), (8, 2, 32, PAD),
        (RANK, COLS), (7, HALF, COLS), (64, COLS), (7, 8, COLS), (8, 64, COLS),
        (RANK, RANK), (RANK, RANK), (8, 128), (8, 128), (8, 8, 128),
    ]
    q, right, squares = pl.pallas_call(
        sums_kernel,
        out_shape=(shape(ROWS, RANK), shape(RANK, COLS), shape(8, 128)),
        in_specs=[VM] * 3,
        out_specs=(VM,) * 3,
        scratch_shapes=[pltpu.VMEM(s, F32) for s in scratch]
        + [pltpu.SemaphoreType.DMA((7,)), pltpu.SemaphoreType.DMA((8,)), pltpu.SemaphoreType.DMA((SEMS,)), pltpu.SemaphoreType.DMA((SEMS,))],
        compiler_params=pltpu.CompilerParams(
            collective_id=0, has_side_effects=True, vmem_limit_bytes=LIMIT
        ),
        name="sums",
    )(momentum, gradient, factor_rows.T)
    new_momentum, update, new_factor = pl.pallas_call(
        outputs_kernel,
        out_shape=(shape(ROWS, COLS), shape(ROWS, COLS), shape(RANK, COLS)),
        in_specs=[VM] * 5,
        out_specs=(VM,) * 3,
        compiler_params=pltpu.CompilerParams(vmem_limit_bytes=LIMIT),
        name="outputs",
    )(momentum, gradient, q, right, squares)
    return new_momentum, update, new_factor.T


def solution(mesh):
    in_specs = (P("fsdp", "tp"), P("fsdp", "tp"), P("tp", None))
    out_specs = (P("fsdp", "tp"), P("fsdp", "tp"), P("tp", None))
    return jax.shard_map(
        per_device, mesh=mesh, in_specs=in_specs, out_specs=out_specs, check_vma=False
    )
```

```python
import math

import jax
import jax.numpy as jnp
from jax import lax
from jax.experimental import pallas as pl
from jax.experimental.pallas import tpu as pltpu
from jax.sharding import PartitionSpec as P

MESH = pl.DeviceIdType.MESH
F32 = jnp.float32
BF16 = jnp.bfloat16
M_ROWS = 7168
N_COLS = 18432
RANK = 448
ROWS = 112
COLS = 1152
HALF = 56
PAD = 512
momentum_decay = 0.95
epsilon = 1e-08

GROUPS = (
    (("x", 0, 384, 1), ("z", 640, 256, 1)),
    (("x", 384, 256, -1), ("z", 896, 256, -1)),
)


def split(a):
    high = a.astype(BF16)
    return high, (a - high.astype(F32)).astype(BF16)


def dot3(a, b, dims):
    ah, al = split(a)
    bh, bl = split(b)

    def one(u, v):
        return lax.dot_general(u, v, (dims, ((), ())), preferred_element_type=F32)

    return one(ah, bh) + (one(ah, bl) + one(al, bh))


def dot_high(a, b, dims):
    return lax.dot_general(
        a, b, (dims, ((), ())), preferred_element_type=F32, precision=lax.Precision.HIGHEST
    )


class Place:
    def __init__(self):
        f, t = lax.axis_index("fsdp"), lax.axis_index("tp")
        eight, two = jnp.int32(8), jnp.int32(2)
        self.at = dict(z=lax.div(f, eight), x=lax.rem(f, eight), y=lax.div(t, two), core=lax.rem(t, two))
        self.steps = {(k, d): lax.rem(v + d, eight) for k, v in self.at.items() for d in range(8)}
        z, x, y, core = (self.at[k] for k in ("z", "x", "y", "core"))
        self.devices = {}
        for d in range(1, 8):
            self.devices["z", d] = (self.steps["z", d] * 8 + x, t)
            self.devices["x", d] = (z * 8 + self.steps["x", d], t)
            self.devices["y", d] = (f, self.steps["y", d] * 2 + core)
        self.devices["core", 1] = (f, y * 2 + 1 - core)

    def device(self, **delta):
        ((axis, d),) = delta.items()
        return self.devices[axis, d % 8]

    def shift(self, at, k):
        return lax.rem(at + (15 - k), jnp.int32(8))

    def step(self, axis, d):
        return self.steps[axis, d % 8]


class Copies:
    def __init__(self, send_sem, recv_sem):
        self.send_sem, self.recv_sem, self.used, self.all = send_sem, recv_sem, 0, []

    def start(self, src, dst, device):
        n = self.used
        self.used += 1
        copy = pltpu.make_async_remote_copy(
            src_ref=src,
            dst_ref=dst,
            send_sem=self.send_sem.at[n],
            recv_sem=self.recv_sem.at[n],
            device_id=device,
            device_id_type=MESH,
        )
        copy.start()
        self.all.append(copy)
        return copy

    def finish(self):
        for copy in self.all:
            copy.wait_send()
        self.all = []


def rows_at(start, size):
    return pl.ds(pl.multiple_of(start, 8), size)


SEMS = 200
ORDER = "iabiabiab"
LATER = "a"
TURNS = {3: "b", 20: "a", 27: "b", 38: "a", 44: "b"}


def sums_kernel(
    mom, grad, fac, q_ref, right_ref, sq_ref,
    pp, pcore, ph, py, pfull, ip, ix, irx, irz, ifull, gp, gr, gs, gd, ga,
    upper, tri, mine, pair, ys, slab_send, slab_recv, send_sem, recv_sem,
):
    here = Place()
    z, x, y, core = (here.at[k] for k in ("z", "x", "y", "core"))
    t = y * 2 + core
    copies = Copies(send_sem, recv_sem)
    barrier = pltpu.get_barrier_semaphore()
    sibling = here.device(core=1)
    peers = [sibling]
    for axis in ("y", "x", "z"):
        peers += [here.device(**{axis: d}) for d in range(1, 8)]
    for peer in peers:
        pl.semaphore_signal(barrier, inc=1, device_id=peer, device_id_type=MESH)
    ip[...] = jnp.zeros((PAD, PAD), F32)
    gs[...] = jnp.zeros((64, COLS), F32)
    pp[:, HALF:] = jnp.zeros((2, 8, RANK), F32)

    buffer = mom[...] + grad[...].astype(F32)
    partial = dot3(buffer, fac[...], ((1,), (1,)))
    pp[0, :HALF] = partial[:HALF]
    pp[1, :HALF] = partial[HALF:]
    pl.semaphore_wait(barrier, len(peers))

    def project():
        copies.start(pp.at[1 - core], pcore, sibling).wait_recv()
        ph[...] = pp[core] + pcore[...]
        cs = []
        for d in range(1, 8):
            cs.append(copies.start(ph.at[rows_at(8 * here.step("y", d), 8)], py.at[d - 1], here.device(y=d)))
        total = ph[rows_at(8 * y, 8), :]
        for d, c in enumerate(cs):
            c.wait_recv()
            total = total + py[d]
        pfull[core, rows_at(8 * y, 8), :] = total
        cs = []
        tile = pfull.at[core, rows_at(8 * y, 8)]
        for d in range(1, 8):
            cs.append(copies.start(tile, tile, here.device(y=d)))
        for c in cs:
            c.wait_recv()
        copies.start(pfull.at[core], pfull.at[core], sibling).wait_recv()
    project()

    projected = jnp.concatenate([pfull[0, :HALF], pfull[1, :HALF], jnp.zeros((16, RANK), F32)], axis=0)
    across = jnp.transpose(projected)
    ip[:RANK, :RANK] = dot_high(across, projected, ((1,), (0,)))

    def chunk(k):
        return (
            rows_at(32 * t + 8 * lax.div(k, jnp.int32(2)), 8),
            pl.ds(pl.multiple_of(256 * lax.rem(k, jnp.int32(2)), 256), 256),
        )

    def inner_sum():
        cs = []
        for d in range(1, 8):
            r, l = chunk(here.step("x", d))
            cs.append(copies.start(ip.at[r, l], irx.at[d - 1], here.device(x=d)))
        yield
        r, l = chunk(x)
        total = ip[r, l]
        for d, c in enumerate(cs):
            c.wait_recv()
            total = total + irx[d]
        ix[...] = total
        cs = [copies.start(ix, irz.at[d - 1], here.device(z=d)) for d in range(1, 8)]
        yield
        for c in cs:
            c.wait_recv()
        total = jnp.zeros((8, 256), F32)
        irz[7] = ix[...]
        for k in range(8):
            total = total + irz[here.shift(z, k)]
        r, l = rows_at(8 * lax.div(x, jnp.int32(2)), 8), pl.ds(pl.multiple_of(256 * lax.rem(x, jnp.int32(2)), 256), 256)
        ifull[y, core, r, l] = total
        part = ifull.at[y, core, r, l]
        cs = [copies.start(part, part, here.device(x=d)) for d in range(1, 8)]
        yield
        for c in cs:
            c.wait_recv()
        each_slab(lambda c: c.start())
        yield

    def slab(place, group, d=1):
        part = ifull.at[place, core, :, pl.ds(128 * group, PAD - 128 * group)]
        return pltpu.make_async_remote_copy(
            src_ref=part,
            dst_ref=part,
            send_sem=slab_send.at[d - 1],
            recv_sem=slab_recv.at[place],
            device_id=here.device(y=d),
            device_id_type=MESH,
        )

    def each_slab(act):
        for group in range(4):

            @pl.when((y >= 2 * group) & (y < min(2 * group + 2, 7)))
            def _():
                for d in range(1, 8):
                    act(slab(y, group, d))

    swaps = {}

    def fetch(j):
        @pl.when(y != j)
        def _():
            slab(j, j // 2).wait_recv()

        part = ifull.at[j, core, :, pl.ds(128 * (j // 2), PAD - 128 * (j // 2))]
        swaps[j] = copies.start(part, part, sibling)

    def block_rows(j):
        swaps[j].wait_recv()
        return ifull[j].reshape(64, PAD)[:, :RANK]

    def outer_sum(group):
        def own(axis, d, ls):
            return gp.at[rows_at(HALF * here.step(axis, d), HALF), ls]

        got = []
        for axis, lane, lanes, way in group:
            ls = pl.ds(lane, lanes)
            got.append({
                (slot, by): copies.start(own(axis, to, ls), gr.at[slot, :, ls], here.device(**{axis: by}))
                for slot, to, by in ((0, 3, 1), (1, -3, -1), (2, 4, 2 * way), (3, 1, 1), (4, -1, -1))
            })
        yield
        for (axis, lane, lanes, way), arrived in zip(group, got):
            ls = pl.ds(lane, lanes)
            for (slot, by), c in arrived.items():
                if slot < 3:
                    c.wait_recv()
            for slot, by in ((0, 2), (1, -2)):
                total = gr[slot, :, ls] + own(axis, by, ls)[...]
                if by == 2 * way:
                    total = total + gr[2, :, ls]
                gr[slot, :, ls] = total
                arrived[slot + 5, by] = copies.start(
                    gr.at[slot, :, ls], gr.at[slot + 5, :, ls], here.device(**{axis: by})
                )
        yield
        cs = {}
        for n, ((axis, lane, lanes, way), arrived) in enumerate(zip(group, got)):
            ls = pl.ds(lane, lanes)
            total = own(axis, 0, ls)[...]
            for (slot, by), c in arrived.items():
                if slot >= 3:
                    c.wait_recv()
                    total = total + gr[slot, :, ls]
            gs[:HALF, ls] = total
            other = "z" if axis == "x" else "x"
            for d in (4, 3, 5, 2, 6, 1, 7):
                src = gs.at[rows_at(8 * here.step(other, d), 8), ls]
                cs[n, d] = copies.start(src, gd.at[d - 1, :, ls], here.device(**{other: d}))
        yield
        back = []
        for n, (axis, lane, lanes, way) in enumerate(group):
            ls = pl.ds(lane, lanes)
            other = "z" if axis == "x" else "x"
            r = rows_at(8 * here.at[other], 8)
            total = gs[r, ls]
            for d in range(1, 8):
                cs[n, d].wait_recv()
                total = total + gd[d - 1, :, ls]
            ga[here.at[axis], r, ls] = total
            part = ga.at[here.at[axis], r, ls]
            back += [copies.start(part, part, here.device(**{other: d})) for d in (4, 3, 5, 2, 6, 1, 7)]
        yield

        def pass_on(axis, place, by, ls):
            part = ga.at[here.step(axis, place), pl.ds(0, HALF), ls]
            return copies.start(part, part, here.device(**{axis: by}))

        for c in back:
            c.wait_recv()
        got = []
        for axis, lane, lanes, way in group:
            got.append([pass_on(axis, 0, by, pl.ds(lane, lanes)) for by in (2, -2, 1, -1)])
        yield
        for (axis, lane, lanes, way), arrived in zip(group, got):
            arrived[0].wait_recv()
            arrived[1].wait_recv()
            for place, by in ((2, -1), (-2, 1), (-2 * way, 2 * way)):
                arrived.append(pass_on(axis, place, by, pl.ds(lane, lanes)))
        yield
        for arrived in got:
            for c in arrived[2:]:
                c.wait_recv()
        yield

    inner_steps, outer_steps = inner_sum(), [outer_sum(group) for group in GROUPS]
    todo = dict(zip("ab", outer_steps))
    todo["i"] = inner_steps
    pa, pb = split(across)
    padded = jnp.concatenate([buffer, jnp.zeros((16, COLS), F32)], axis=0)
    bh, bl = split(padded)

    def one(u, v):
        return jnp.dot(u, v, preferred_element_type=F32)

    next(inner_steps)
    for n, group in enumerate(GROUPS):
        for axis, lane, lanes, way in group:
            ls = slice(lane, lane + lanes)
            gp[:, ls] = one(pa, bh[:, ls]) + (one(pa, bl[:, ls]) + one(pb, bh[:, ls]))
        next(outer_steps[n])
    for name in ORDER:
        next(todo[name])
    fetch(0)
    for name in LATER:
        next(todo[name])
    ready = 64 * 6

    def grown(size):
        return jnp.concatenate([ga[k, :HALF] for k in range(8)], axis=0)[:size]

    for n, _ in enumerate(factor(block_rows, upper, tri)):
        if n % 8 == 3 and n < 48:
            fetch(n // 8 + 1)
        if n in TURNS:
            next(todo[TURNS[n]])
        if n == 48:
            right_ref[:ready] = dot3(tri[:ready, :ready], grown(ready), ((1,), (0,)))
    right_ref[ready:] = dot3(tri[ready:], grown(RANK), ((1,), (0,)))
    inverse, right = tri[...], right_ref[...]
    total = right[:, :128] * right[:, :128]
    for k in range(1, 9):
        total = total + right[:, 128 * k : 128 * (k + 1)] * right[:, 128 * k : 128 * (k + 1)]
    total = jnp.concatenate([total, jnp.zeros((PAD - RANK, 128), F32)], axis=0)
    total = jnp.sum(jnp.transpose(total), axis=0, keepdims=True)
    mine[...] = jnp.concatenate(
        [total[:, 128 * k : 128 * (k + 1)] for k in range(4)] + [jnp.zeros((4, 128), F32)], axis=0
    )
    c = copies.start(mine, pair, sibling)
    c.wait_recv()
    ys[7] = mine[...] + pair[...]
    cs = [copies.start(ys.at[7], ys.at[d - 1], here.device(y=d)) for d in range(1, 8)]
    q_ref[...] = dot3(projected[:ROWS], inverse, ((1,), (1,)))
    copies.finish()

    each_slab(lambda c: c.wait_send())
    for c in cs:
        c.wait_recv()
    total = jnp.zeros((8, 128), F32)
    for k in range(8):
        total = total + ys[here.shift(y, k)]
    sq_ref[...] = total
    copies.finish()


def factor_block(block):
    row = lax.broadcasted_iota(jnp.int32, (64, 64), 0)
    col = lax.broadcasted_iota(jnp.int32, (64, 64), 1)
    diagonal = jnp.where(row == col, block, 0.0)
    across = lax.rsqrt(jnp.sum(diagonal, axis=0, keepdims=True))
    block = block * lax.rsqrt(jnp.sum(diagonal, axis=1, keepdims=True)) * across
    rest = jnp.concatenate([block, jnp.where(row == col, 1.0, 0.0).astype(F32)], axis=1)
    done = []
    for p in range(8):
        n = 64 - 8 * p
        below = lax.broadcasted_iota(jnp.int32, (n, 128), 0)
        cols = jnp.stack([jnp.broadcast_to(rest[:, 8 * p + k : 8 * p + k + 1], (n, 128)) for k in range(8)])
        for k in range(0, 8, 2):
            first, both, second = cols[0, k : k + 1], cols[1, k : k + 1], cols[1, k + 1 : k + 2]
            root = lax.rsqrt(first)
            root2 = lax.rsqrt(first * second - both * both) * (first * root)
            inverse = root * root
            ratio = both * inverse
            m = jnp.where(below > k, cols[0] * inverse, 0.0)
            m2 = jnp.where(below > k + 1, (cols[1] - m * both) * (root2 * root2), 0.0)
            line = rest[k : k + 1]
            line2 = rest[k + 1 : k + 2] - ratio * line
            done += [line * root, line2 * root2]
            rest = rest - m * line - m2 * line2
            if k < 6:
                lead = cols[2:, k : k + 1]
                lead2 = cols[2:, k + 1 : k + 2] - ratio * lead
                cols = cols[2:] - m[None] * lead - m2[None] * lead2
        rest = rest[8:]
        yield None
    yield jnp.concatenate(done, axis=0)[:, 64:] * across


def factor(block_rows, upper, tri):
    lanes = lax.broadcasted_iota(jnp.int32, (64, RANK), 1)
    for j in range(7):
        lo, hi = 64 * j, 64 * (j + 1)
        block = block_rows(j)
        if j > 0:
            before = lax.broadcasted_iota(jnp.int32, (lo, RANK), 1)
            down = jnp.where(before < lo, tri[:lo, :], upper[:lo, :])
            block = jnp.where(lanes < lo, 0.0, block) - dot_high(upper[:lo, lo:hi], down, ((0,), (0,)))
        for both in factor_block(block[:, lo:hi]):
            if both is None:
                yield None
        inverse = both
        rows = dot_high(inverse, block, ((1,), (0,)))
        upper[lo:hi, :] = rows
        parts = [inverse]
        if j > 0:
            parts.insert(0, rows[:, :lo])
        if j < 6:
            parts.append(jnp.zeros((64, RANK - hi), F32))
        tri[lo:hi, :] = jnp.concatenate(parts, axis=1)


def outputs_kernel(mom_ref, grad_ref, q_ref, right_ref, sq_ref, nm_ref, up_ref, nf_ref):
    inverse = lax.rsqrt(sq_ref[...] + epsilon)
    inverse = jnp.concatenate([inverse[k : k + 1] for k in range(4)], axis=1)
    column = jnp.transpose(jnp.broadcast_to(inverse, (128, PAD)))[:RANK, 0:1]
    right = right_ref[...]
    nf_ref[...] = right * column
    rh, rl = split(right)
    q = q_ref[...]
    scale_factor = math.sqrt(M_ROWS * N_COLS / RANK)
    qh, ql = split(q * (scale_factor * inverse[:, :RANK]))

    def one(u, v):
        return jnp.dot(u, v, preferred_element_type=F32)

    up_ref[...] = one(qh, rh) + (one(qh, rl) + one(ql, rh))
    buffer = mom_ref[...] + grad_ref[...].astype(F32)
    nm_ref[...] = buffer - one((q * (1.0 - momentum_decay)).astype(BF16), rh)


def shape(*dims):
    return jax.ShapeDtypeStruct(dims, F32)


VM = pl.BlockSpec(memory_space=pltpu.VMEM)
LIMIT = 48 * 1024 * 1024


def per_device(momentum, gradient, factor_rows):
    scratch = [
        (2, 64, RANK), (64, RANK), (64, RANK), (7, 8, RANK), (2, 64, RANK),
        (PAD, PAD), (8, 256), (7, 8, 256), (8, 8, 256), (8, 2, 32, PAD),
        (RANK, COLS), (7, HALF, COLS), (64, COLS), (7, 8, COLS), (8, 64, COLS),
        (RANK, RANK), (RANK, RANK), (8, 128), (8, 128), (8, 8, 128),
    ]
    q, right, squares = pl.pallas_call(
        sums_kernel,
        out_shape=(shape(ROWS, RANK), shape(RANK, COLS), shape(8, 128)),
        in_specs=[VM] * 3,
        out_specs=(VM,) * 3,
        scratch_shapes=[pltpu.VMEM(s, F32) for s in scratch]
        + [pltpu.SemaphoreType.DMA((7,)), pltpu.SemaphoreType.DMA((8,)), pltpu.SemaphoreType.DMA((SEMS,)), pltpu.SemaphoreType.DMA((SEMS,))],
        compiler_params=pltpu.CompilerParams(
            collective_id=0, has_side_effects=True, vmem_limit_bytes=LIMIT
        ),
        name="sums",
    )(momentum, gradient, factor_rows.T)
    new_momentum, update, new_factor = pl.pallas_call(
        outputs_kernel,
        out_shape=(shape(ROWS, COLS), shape(ROWS, COLS), shape(RANK, COLS)),
        in_specs=[VM] * 5,
        out_specs=(VM,) * 3,
        compiler_params=pltpu.CompilerParams(vmem_limit_bytes=LIMIT),
        name="outputs",
    )(momentum, gradient, q, right, squares)
    return new_momentum, update, new_factor.T


def solution(mesh):
    in_specs = (P("fsdp", "tp"), P("fsdp", "tp"), P("tp", None))
    out_specs = (P("fsdp", "tp"), P("fsdp", "tp"), P("tp", None))
    return jax.shard_map(
        per_device, mesh=mesh, in_specs=in_specs, out_specs=out_specs, check_vma=False
    )
```
